32 devices in a mesh: groups: 2 (over y), rows: 4 (over z), cols: 2 (over x), date: 2 (over core).
Axes of the slice: x: 2, y: 2, z: 4, core: 2. Of those that a mesh axis runs over, the one named last changes fastest.
Arguments:
- features: bfloat16 [2, 128, 256, 128], P('date', ('groups', 'rows'), 'cols'), parts along dimension 1, may hold values from -6 to 6
- scene_shift: int32 [8, 2, 2], P('groups'), parts along dimension 0, may hold values from -4 to 4, as said below
- w_lat: bfloat16 [128, 128], replicated, may hold values from -0.5 to 0.5
- b_lat: float32 [128], replicated, may hold values from -3 to 3
- w_fpn: bfloat16 [3, 3, 128, 128], replicated, may hold values from -0.1875 to 0.1875
- w_dec1: bfloat16 [3, 3, 128, 128], replicated, may hold values from -0.1875 to 0.1875
- b_dec1: float32 [128], replicated, may hold values from -3 to 3
- w_dec2: bfloat16 [3, 3, 128, 128], replicated, may hold values from -0.1875 to 0.1875
- b_dec2: float32 [128], replicated, may hold values from -3 to 3
- w_out: bfloat16 [128], replicated, may hold values from -0.5 to 0.5
- b_out: float32 [1], replicated, may hold values from -3 to 3
Outputs:
- change_logit: float32 [128, 256], P(('groups', 'rows', 'date'), 'cols'), parts along dimension 0
The draws below stay inside these ranges and needn't reach their ends.
There are 2 independent parts, one for each index of `groups`. The reference program is written for one: setup_inputs(seed, part) draws one part's arguments, and reference() takes and returns one part's arrays. A program takes and returns all parts, laid end to end along the dimension named above; an argument that names none is the same for every part. Nothing has to cross between parts.
Inputs may be any that keep to these rules, and one draw needn't show every extreme that they name: `scene_shift`: each offset component lies between -4 and 4; 4 and -4 both occur in every draw.
All inputs are finite; a program needn't handle non-finite values.
Results may differ from the reference program's by a relative error of at most 0.0076.
Values may be sent and summed in bfloat16 or wider, within the bound.
A program may use at most 64 MiB of HBM per device.

```python
import jax
import jax.numpy as jnp
from jax import lax

C = 128
CIN = 128
TH = 16
TW = 128
MO = 4
TILE_ROWS = 4
TILE_COLS = 2
GH = 64
GW = 256


def draw_scene_shift(key, part):
    base = jax.random.randint(key, (TILE_ROWS, TILE_COLS, 2), -MO, MO + 1).astype(jnp.int32)
    pick_row = jax.random.randint(jax.random.fold_in(key, 7), (), 0, TILE_ROWS)
    pick_col = jax.random.randint(jax.random.fold_in(key, 8), (), 0, TILE_COLS)
    base = base.at[pick_row, pick_col].set(jnp.array([MO, -MO], jnp.int32))
    other_row = (pick_row + TILE_ROWS // 2) % TILE_ROWS
    base = base.at[other_row, pick_col].set(jnp.array([-MO, MO], jnp.int32))
    return base


def levels(own_key, extent, pieces, low, top_value):
    level, own = 1.0, jax.random.fold_in(own_key, 6)
    for axis_at, blocks in pieces:
        steps = jnp.exp(jax.random.uniform(jax.random.fold_in(own, axis_at), (blocks,), jnp.float32, low / len(pieces), top_value / len(pieces)))
        level = level * jnp.repeat(steps, extent[axis_at] // blocks).reshape([-1 if axis == axis_at else 1 for axis in range(len(extent))])
    return level


def scatter_about(own_key, dims, deviation, most, shards=(), held_as=jnp.bfloat16):
    drawn = deviation * jax.random.normal(own_key, dims, jnp.float32)
    if shards:
        drawn = drawn * levels(own_key, dims, shards, -0.22, 0.18)
    return jnp.clip(drawn, -most, most).astype(held_as)


def setup_inputs(seed: int = 0, part: int = 0) -> dict:
    keys = jax.random.split(jax.random.key(seed), 12)
    part_keys = jax.random.split(jax.random.fold_in(keys[11], part), 12)
    return {
        "features": scatter_about(part_keys[0], (2, GH, GW, CIN), 1.0, 6.0, ((0, 2), (1, 4), (2, 2))),
        "scene_shift": draw_scene_shift(jax.random.fold_in(jax.random.fold_in(keys[11], part), 71), part),
        "w_lat": scatter_about(keys[2], (CIN, C), CIN ** -0.5, 0.5),
        "b_lat": scatter_about(keys[3], (C,), 0.5, 3.0, (), jnp.float32),
        "w_fpn": scatter_about(keys[4], (3, 3, C, C), (9 * C) ** -0.5, 0.1875),
        "w_dec1": scatter_about(keys[5], (3, 3, C, C), (9 * C) ** -0.5, 0.1875),
        "b_dec1": scatter_about(keys[6], (C,), 0.5, 3.0, (), jnp.float32),
        "w_dec2": scatter_about(keys[7], (3, 3, C, C), (9 * C) ** -0.5, 0.1875),
        "b_dec2": scatter_about(keys[8], (C,), 0.5, 3.0, (), jnp.float32),
        "w_out": scatter_about(keys[9], (C,), C ** -0.5, 0.5),
        "b_out": scatter_about(keys[10], (1,), 1.0, 3.0, (), jnp.float32),
    }


def conv_three(padded, weights):
    out_rows = padded.shape[0] - 2
    out_cols = padded.shape[1] - 2
    channels = padded.shape[2]
    total = jnp.zeros((out_rows * out_cols, weights.shape[3]), jnp.float32)
    for row_tap in range(3):
        for col_tap in range(3):
            window = padded[row_tap:row_tap + out_rows, col_tap:col_tap + out_cols].reshape(-1, channels)
            total = total + jnp.dot(window, weights[row_tap, col_tap], preferred_element_type=jnp.float32)
    return total.reshape(out_rows, out_cols, weights.shape[3])


def pad_one(field):
    return jnp.pad(field, ((1, 1), (1, 1), (0, 0)))


def reference(features, scene_shift, w_lat, b_lat, w_fpn, w_dec1, b_dec1, w_dec2, b_dec2, w_out, b_out):
    rows_all = features.shape[1]
    cols_all = features.shape[2]
    lateral = (jnp.dot(features.reshape(-1, CIN), w_lat, preferred_element_type=jnp.float32) + b_lat).astype(jnp.bfloat16)
    lateral = lateral.reshape(2, rows_all, cols_all, C)
    pyramid_a = conv_three(pad_one(lateral[0]), w_fpn).astype(jnp.bfloat16)
    pyramid_b = conv_three(pad_one(lateral[1]), w_fpn).astype(jnp.bfloat16)
    canvas = jnp.zeros((rows_all + 2 * MO, cols_all + 2 * MO, C), jnp.float32)
    counts = jnp.zeros((rows_all + 2 * MO, cols_all + 2 * MO), jnp.float32)

    def place(index, carry):
        canvas, counts = carry
        index = jnp.asarray(index).astype(jnp.int32)
        scene_row = index // TILE_COLS
        scene_col = index % TILE_COLS
        top = (scene_row * TH + scene_shift[scene_row, scene_col, 0] + MO).astype(jnp.int32)
        left = (scene_col * TW + scene_shift[scene_row, scene_col, 1] + MO).astype(jnp.int32)
        zero = jnp.zeros((), jnp.int32)
        piece = lax.dynamic_slice(pyramid_b, ((scene_row * TH).astype(jnp.int32), (scene_col * TW).astype(jnp.int32), zero), (TH, TW, C)).astype(jnp.float32)
        region = lax.dynamic_slice(canvas, (top, left, zero), (TH, TW, C))
        canvas = lax.dynamic_update_slice(canvas, region + piece, (top, left, zero))
        region_count = lax.dynamic_slice(counts, (top, left), (TH, TW))
        counts = lax.dynamic_update_slice(counts, region_count + jnp.float32(1.0), (top, left))
        return canvas, counts

    canvas, counts = lax.fori_loop(0, TILE_ROWS * TILE_COLS, place, (canvas, counts))
    b_sum = canvas[MO:MO + rows_all, MO:MO + cols_all]
    coverage = counts[MO:MO + rows_all, MO:MO + cols_all]
    regridded = b_sum / jnp.maximum(coverage, 1.0)[:, :, None]
    covered = jnp.minimum(coverage, 1.0)[:, :, None]
    difference = (jnp.abs(pyramid_a.astype(jnp.float32) - regridded) * covered).astype(jnp.bfloat16)
    hidden_one = jnp.maximum(conv_three(pad_one(difference), w_dec1) + b_dec1, 0.0).astype(jnp.bfloat16)
    hidden_two = jnp.maximum(conv_three(pad_one(hidden_one), w_dec2) + b_dec2, 0.0).astype(jnp.bfloat16)
    logit = jnp.dot(hidden_two.reshape(-1, C), w_out, preferred_element_type=jnp.float32) + b_out
    return logit.reshape(rows_all, cols_all)
```

```python
import functools

import jax
import jax.numpy as jnp
from jax import lax
from jax.experimental import pallas as pl
from jax.experimental.pallas import tpu as pltpu
from jax.sharding import PartitionSpec as P

MO = 4
HALO = (3, 2 + MO + 1)
SIDE = 16
MESH = pl.DeviceIdType.MESH
F32 = jnp.float32
BF16 = jnp.bfloat16


def kernel(
    sizes,
    feat,
    shift_ref,
    w_lat,
    b_lat,
    w_fpn,
    w_dec1,
    b_dec1,
    w_dec2,
    b_dec2,
    w_out,
    b_out,
    out_ref,
    field,
    lat6,
    pyr_a,
    pyr_b,
    dif6,
    hid6,
    wl2,
    wf2,
    wd1,
    wd2,
    send_sem,
    recv_sem,
    copy_sem,
):
    row_tiles, col_tiles, tile_rows, tile_cols = sizes
    half = tile_rows // 2
    wide = tile_cols + 2 * SIDE
    mid = tile_cols + SIDE
    rows_of = tuple(half + 2 * h for h in HALO)
    base_of = (0, rows_of[0])
    ch = feat.shape[2]
    r = lax.axis_index("rows")
    c = lax.axis_index("cols")
    d = lax.axis_index("date")
    upper = d == 0
    has_col = {0: c >= 0, 1: c + 1 < col_tiles, -1: c >= 1}
    has_down = r + 1 < row_tiles
    has_up = r >= 1
    other_row = jnp.where(upper, r - 1, r + 1)
    has_other = (other_row >= 0) & (other_row < row_tiles)

    def local(src, dst, index):
        copy = pltpu.make_async_copy(src, dst, copy_sem.at[index])
        copy.start()
        return copy

    depth = 9 * ch
    lat_copies = [
        local(w_lat, wl2.at[pl.ds(0, ch), pl.ds(0, ch)], 0),
        local(w_lat, wl2.at[pl.ds(ch, ch), pl.ds(ch, ch)], 1),
    ]
    conv_copies = []
    for at, (src, dst) in enumerate(((w_fpn, wf2), (w_dec1, wd1), (w_dec2, wd2))):
        conv_copies.append(
            (
                local(src, dst.at[pl.ds(0, depth), pl.ds(0, ch)], 2 + 2 * at),
                local(src, dst.at[pl.ds(3 * ch, depth), pl.ds(ch, ch)], 3 + 2 * at),
            )
        )

    barrier = pltpu.get_barrier_semaphore()
    for step in (0, 1, -1):
        for date in (0, 1):
            here = has_col[step] if step else d != date

            @pl.when(here)
            def _():
                pl.semaphore_signal(
                    barrier,
                    inc=1,
                    device_id={"rows": r, "cols": c + step, "date": date},
                    device_id_type=MESH,
                )

            @pl.when(has_col[step] & has_other)
            def _():
                pl.semaphore_signal(
                    barrier,
                    inc=1,
                    device_id={"rows": other_row, "cols": c + step, "date": date},
                    device_id_type=MESH,
                )

    wl2[0:ch, ch:] = jnp.zeros((ch, ch), BF16)
    wl2[ch:, 0:ch] = jnp.zeros((ch, ch), BF16)
    for dst in (wf2, wd1, wd2):
        dst[depth:, 0:ch] = jnp.zeros((3 * ch, ch), BF16)
        dst[0 : 3 * ch, ch:] = jnp.zeros((3 * ch, ch), BF16)

    def start_row(date, place, kind):
        own = HALO[date] if place == 0 else 0
        other = 0 if place == 0 else half + HALO[date]
        return base_of[date] + (own if kind == 0 else other)

    for place in (0, 1):

        @pl.when((d == place) & jnp.logical_not(has_other))
        def _():
            for date in (0, 1):
                first = start_row(date, place, 1)
                field[first : first + HALO[date]] = jnp.zeros((HALO[date], wide, ch), BF16)

    cols_beside = jnp.where(has_col[1], 1, 0) + jnp.where(has_col[-1], 1, 0) + 1
    rows_beside = jnp.where(has_down, 1, 0) + jnp.where(has_up, 1, 0)
    pl.semaphore_wait(barrier, (2 + rows_beside) * cols_beside - 1)

    def pieces(date):
        h = HALO[date]
        found = []
        for rk, (row_step, place, ok) in enumerate(
            (
                (0, 1 - date, None),
                (0, date, None),
                (1, 0, has_down),
                (-1, 1, has_up),
            )
        ):
            kind = 0 if row_step == 0 else 1
            count = half + h if kind == 0 else h
            if kind == 0:
                src_row = 0 if place == 0 else half - h
            else:
                src_row = tile_rows - h if place == 0 else 0
            dst_row = start_row(date, place, kind)
            for ck, step in enumerate((0, 1, -1)):
                if rk == 1 and step == 0:
                    continue
                src_col, dst_col, width = (
                    (0, SIDE, tile_cols),
                    (tile_cols - SIDE, 0, SIDE),
                    (0, SIDE + tile_cols, SIDE),
                )[ck]
                go = has_col[step]
                if ok is not None:
                    go = go & ok
                copy = pltpu.make_async_remote_copy(
                    src_ref=feat.at[pl.ds(src_row, count), pl.ds(src_col, width)],
                    dst_ref=field.at[pl.ds(dst_row, count), pl.ds(dst_col, width)],
                    send_sem=send_sem.at[rk, ck],
                    recv_sem=recv_sem.at[date, kind, ck],
                    device_id={"rows": r + row_step, "cols": c + step, "date": place},
                    device_id_type=MESH,
                )
                found.append(((kind, -abs(step)), go, copy))
        found.sort(key=lambda item: item[0])
        return [item[1:] for item in found]

    def own_copy(date):
        h = HALO[date]
        return pltpu.make_async_copy(
            feat.at[pl.ds(0 if date == 0 else half - h, half + h)],
            field.at[pl.ds(start_row(date, date, 0), half + h), pl.ds(SIDE, tile_cols)],
            recv_sem.at[date, 0, 0],
        )

    for date in (0, 1):

        @pl.when(d == date)
        def _():
            for go, copy in pieces(date):

                @pl.when(go)
                def _():
                    copy.start()

            own_copy(date).start()

    def await_kind(kind):
        for date in (0, 1):
            h = HALO[date]
            count = half + h if kind == 0 else h
            first = jnp.where(upper, start_row(date, 0, kind), start_row(date, 1, kind))
            for ck, step in enumerate((0, -1, 1)):
                dst_col, width = ((SIDE, tile_cols), (0, SIDE), (SIDE + tile_cols, SIDE))[ck]
                view = field.at[pl.ds(first, count), pl.ds(dst_col, width)]

                def wait():
                    pltpu.make_async_copy(view, view, recv_sem.at[date, kind, ck]).wait()

                ok = has_col[step]
                if kind == 1:
                    ok = ok & has_other
                pl.when(ok)(wait)

    far = 1 << 20
    origin = (2 * r + d) * half
    rows_total = row_tiles * tile_rows
    left_end = -c * tile_cols
    right_end = (col_tiles - c) * tile_cols
    x_wide = lax.broadcasted_iota(jnp.int32, (wide, ch), 0) - SIDE
    x_mid = lax.broadcasted_iota(jnp.int32, (mid, ch), 0) - SIDE // 2
    edge = SIDE // 2

    def inside(x, y):
        row = origin + y
        end = jnp.where((row >= 0) & (row < rows_total), right_end, -far)
        return (x >= left_end) & (x < end)

    def put_taps(dst, pair, slot, value, lo, hi):
        total = value.shape[0]
        at = slot * 3 * ch
        taps = (pltpu.roll(value, 1, 0), value, pltpu.roll(value, total - 1, 0))
        for tap, moved in enumerate(taps):
            dst[pair, :, at + tap * ch : at + (tap + 1) * ch] = moved[lo:hi].astype(BF16)

    lat_bias = b_lat[...]

    def lateral_pair(date, q):
        first = base_of[date] + 2 * q
        both = jnp.concatenate([field[first], field[first + 1]], axis=-1)
        value = jnp.dot(both, wl2[...], preferred_element_type=F32)
        for slot in (0, 1):
            y = 2 * q + slot - HALO[date]
            part = value[:, slot * ch : (slot + 1) * ch] + lat_bias
            part = jnp.where(inside(x_wide, y), part, 0.0)
            put_taps(lat6, base_of[date] // 2 + q, slot, part, edge, wide - edge)

    def conv_pairs(src, weights, first, count):
        width, deep = src.shape[1:]
        top = src[pl.ds(first, count)].reshape(count * width, deep)
        low = src[pl.ds(first + 1, count)].reshape(count * width, deep)
        return jnp.dot(top, weights[0:deep], preferred_element_type=F32) + jnp.dot(
            low, weights[deep:], preferred_element_type=F32
        )

    def pyramid_pairs(date, q, count):
        value = conv_pairs(lat6, wf2, base_of[date] // 2 + q, count)
        value = value.astype(BF16).astype(F32)
        for pair in range(count):
            for slot in (0, 1):
                part = value[pair * mid : (pair + 1) * mid, slot * ch : (slot + 1) * ch]
                if date == 0:
                    pyr_a[2 * (q + pair) + slot] = part
                else:
                    pyr_b[2 * (q + pair) + slot, edge : edge + mid] = part

    def phase(kind):
        for date in (0, 1):
            pairs = rows_of[date] // 2
            late = (HALO[date] + 1) // 2
            count = pairs - late if kind == 0 else late
            low_first = 0 if kind == 0 else pairs - late
            first = jnp.where(upper, pairs - count - low_first, low_first)

            def body(i, carry):
                lateral_pair(date, first + i)
                return carry

            lax.fori_loop(0, count, body, 0)
        if kind == 0:
            for copy in conv_copies[0]:
                copy.wait()
        for date in (0, 1):
            pairs = rows_of[date] // 2 - 1
            late = (HALO[date] + 1) // 2
            count = pairs - late if kind == 0 else late
            low_first = 0 if kind == 0 else pairs - late
            first = jnp.where(upper, pairs - count - low_first, low_first)

            def body(i, carry):
                pyramid_pairs(date, first + 2 * i, 2)
                return carry

            lax.fori_loop(0, count // 2, body, 0)

    for copy in lat_copies:
        copy.wait()
    await_kind(0)
    phase(0)
    await_kind(1)
    phase(1)

    tiles = []
    for kind in (0, 1):
        tile_row = r if kind == 0 else jnp.clip(other_row, 0, row_tiles - 1)
        for step in (0, -1, 1):
            tile = tile_row * col_tiles + jnp.clip(c + step, 0, col_tiles - 1)
            ok = has_col[step]
            if kind == 1:
                ok = ok & has_other
            tiles.append((kind, step, ok, shift_ref[2 * tile], shift_ref[2 * tile + 1]))
    reach = HALO[1] - 1
    x_left = x_mid[0:SIDE]
    x_right = x_mid[mid - SIDE : mid]

    def regrid_row(p, slot):
        y = 2 * p + slot - 2
        sums = {0: 0.0, -1: 0.0, 1: 0.0}
        seen = {0: 0.0, -1: 0.0, 1: 0.0}
        for kind, step, ok, row_by, col_by in tiles:
            u = y + d * half - row_by
            within = (u >= 0) & (u < tile_rows)
            use = ok & (within if kind == 0 else jnp.logical_not(within))
            if step == 0:
                x, start, size = x_mid, 0, mid
                low, high = col_by, tile_cols + col_by
            elif step == -1:
                x, start, size = x_left, 0, SIDE
                low, high = -far, col_by
            else:
                x, start, size = x_right, mid - SIDE, SIDE
                low, high = tile_cols + col_by, far
            mask = (x >= low) & (x < jnp.where(use, high, -2 * far))
            piece = pyr_b[y - row_by + reach, pl.ds(start + edge - col_by, size), :]
            sums[step] = sums[step] + jnp.where(mask, piece, 0.0)
            seen[step] = seen[step] + jnp.where(mask, 1.0, 0.0)

        def whole(parts):
            full = parts[0]
            return jnp.concatenate(
                [
                    full[0:SIDE] + parts[-1],
                    full[SIDE : mid - SIDE],
                    full[mid - SIDE :] + parts[1],
                ],
                axis=0,
            )

        total, cover = whole(sums), whole(seen)
        placed = total / jnp.maximum(cover, 1.0)
        diff = jnp.abs(pyr_a[2 * p + slot] - placed) * jnp.minimum(cover, 1.0)
        diff = jnp.where(inside(x_mid, y), diff, 0.0)
        put_taps(dif6, p, slot, diff, 0, mid)

    def regrid_body(p, carry):
        regrid_row(p, 0)
        regrid_row(p, 1)
        return carry

    lax.fori_loop(0, half // 2 + 2, regrid_body, 0)

    for copy in conv_copies[1]:
        copy.wait()
    bias_one = b_dec1[...]

    def dec_one(i, carry):
        value = conv_pairs(dif6, wd1, i, 1)
        for slot in (0, 1):
            part = jnp.maximum(value[:, slot * ch : (slot + 1) * ch] + bias_one, 0.0)
            part = jnp.where(inside(x_mid, 2 * i + slot - 1), part, 0.0)
            put_taps(hid6, i, slot, part, edge, mid - edge)
        return carry

    lax.fori_loop(0, half // 2 + 1, dec_one, 0)

    for copy in conv_copies[2]:
        copy.wait()
    bias_two = b_dec2[...]
    out_w = jnp.broadcast_to(w_out[...].astype(F32), (16, ch)).astype(BF16)
    out_b = b_out[0]
    for i in range(0, half // 2, 2):
        value = conv_pairs(hid6, wd2, i, 2)
        for pair in (0, 1):
            for slot in (0, 1):
                part = value[pair * tile_cols : (pair + 1) * tile_cols, slot * ch : (slot + 1) * ch]
                part = jnp.maximum(part + bias_two, 0.0).astype(BF16)
                logit = lax.dot_general(
                    out_w, part, (((1,), (1,)), ((), ())), preferred_element_type=F32
                )
                y = 2 * (i + pair) + slot
                out_ref[y : y + 1, :] = logit[0:1] + out_b

    for date in (0, 1):

        @pl.when(d == date)
        def _():
            for go, copy in pieces(date):

                @pl.when(go)
                def _():
                    copy.wait_send()


def per_device(
    features, scene_shift, w_lat, b_lat, w_fpn, w_dec1, b_dec1, w_dec2, b_dec2, w_out, b_out
):
    tile_rows, tile_cols, ch = features.shape[1:]
    half = tile_rows // 2
    sizes = (lax.axis_size("rows"), lax.axis_size("cols"), tile_rows, tile_cols)
    rows_of = tuple(half + 2 * h for h in HALO)
    wide, mid = tile_cols + 2 * SIDE, tile_cols + SIDE
    any_spec = pl.BlockSpec(memory_space=pl.ANY)
    vmem = pl.BlockSpec(memory_space=pltpu.VMEM)
    smem = pl.BlockSpec(memory_space=pltpu.SMEM)
    flops = 2 * ch * ch * tile_cols * 9 * 60
    return pl.pallas_call(
        functools.partial(kernel, sizes),
        out_shape=jax.ShapeDtypeStruct((half, tile_cols), F32),
        in_specs=[
            any_spec,
            smem,
            any_spec,
            vmem,
            any_spec,
            any_spec,
            vmem,
            any_spec,
            vmem,
            vmem,
            smem,
        ],
        out_specs=vmem,
        scratch_shapes=[
            pltpu.VMEM((sum(rows_of), wide, ch), BF16),
            pltpu.VMEM((sum(rows_of) // 2, mid, 6 * ch), BF16),
            pltpu.VMEM((half + 4, mid, ch), F32),
            pltpu.VMEM((half + 2 * HALO[1] - 2, wide, ch), F32),
            pltpu.VMEM((half // 2 + 2, mid, 6 * ch), BF16),
            pltpu.VMEM((half // 2 + 1, tile_cols, 6 * ch), BF16),
            pltpu.VMEM((2 * ch, 2 * ch), BF16),
            pltpu.VMEM((12 * ch, 2 * ch), BF16),
            pltpu.VMEM((12 * ch, 2 * ch), BF16),
            pltpu.VMEM((12 * ch, 2 * ch), BF16),
            pltpu.SemaphoreType.DMA((4, 3)),
            pltpu.SemaphoreType.DMA((2, 2, 3)),
            pltpu.SemaphoreType.DMA((8,)),
        ],
        compiler_params=pltpu.CompilerParams(
            collective_id=0, has_side_effects=True, vmem_limit_bytes=48 << 20
        ),
        cost_estimate=pl.CostEstimate(flops=flops, bytes_accessed=4 << 20, transcendentals=0),
    )(
        features[0],
        scene_shift.reshape(-1),
        w_lat,
        b_lat.reshape(1, ch),
        w_fpn.reshape(9 * ch, ch),
        w_dec1.reshape(9 * ch, ch),
        b_dec1.reshape(1, ch),
        w_dec2.reshape(9 * ch, ch),
        b_dec2.reshape(1, ch),
        w_out.reshape(1, ch),
        b_out,
    )


def solution(mesh):
    return jax.shard_map(
        per_device,
        mesh=mesh,
        in_specs=(
            P("date", ("groups", "rows"), "cols", None),
            P("groups", None, None),
            P(),
            P(),
            P(),
            P(),
            P(),
            P(),
            P(),
            P(),
            P(),
        ),
        out_specs=P(("groups", "rows", "date"), "cols"),
        check_vma=False,
    )
```

```python
import functools

import jax
import jax.numpy as jnp
from jax import lax
from jax.experimental import pallas as pl
from jax.experimental.pallas import tpu as pltpu
from jax.sharding import PartitionSpec as P

MO = 4
HALO = (3, 2 + MO + 1)
SIDE = 8
MESH = pl.DeviceIdType.MESH
F32 = jnp.float32
BF16 = jnp.bfloat16


def kernel(
    sizes,
    feat,
    shift_ref,
    w_lat,
    b_lat,
    w_fpn,
    w_dec1,
    b_dec1,
    w_dec2,
    b_dec2,
    w_out,
    b_out,
    out_ref,
    field,
    lat6,
    pyr_a,
    pyr_b,
    dif6,
    hid6,
    wl2,
    wf2,
    wd1,
    wd2,
    vec_lat,
    vec_one,
    vec_two,
    vec_out,
    send_sem,
    recv_sem,
    copy_sem,
):
    row_tiles, col_tiles, tile_rows, tile_cols = sizes
    half = tile_rows // 2
    mid = tile_cols + 2 * SIDE
    groups = mid // SIDE
    core = tile_cols // SIDE
    rows_of = tuple(half + 2 * h for h in HALO)
    base_of = (0, rows_of[0])
    ch = feat.shape[3]
    r = lax.axis_index("rows")
    c = lax.axis_index("cols")
    d = lax.axis_index("date")
    upper = d == 0
    has_col = {0: c >= 0, 1: c + 1 < col_tiles, -1: c >= 1}
    has_down = r + 1 < row_tiles
    has_up = r >= 1
    other_row = jnp.where(upper, r - 1, r + 1)
    has_other = (other_row >= 0) & (other_row < row_tiles)

    def local(src, dst, index):
        copy = pltpu.make_async_copy(src, dst, copy_sem.at[index])
        copy.start()
        return copy

    depth = 9 * ch
    lat_copies = [
        local(w_lat, wl2.at[pl.ds(0, ch), pl.ds(0, ch)], 0),
        local(w_lat, wl2.at[pl.ds(ch, ch), pl.ds(ch, ch)], 1),
    ]
    lat_copies.append(local(b_lat, vec_lat, 8))
    conv_copies = []
    for at, (src, dst) in enumerate(((w_fpn, wf2), (w_dec1, wd1), (w_dec2, wd2))):
        conv_copies.append(
            [
                local(src, dst.at[pl.ds(0, depth), pl.ds(0, ch)], 2 + 2 * at),
                local(src, dst.at[pl.ds(3 * ch, depth), pl.ds(ch, ch)], 3 + 2 * at),
            ]
        )
    conv_copies[1].append(local(b_dec1, vec_one, 9))
    conv_copies[2].append(local(b_dec2, vec_two, 10))
    conv_copies[2].append(local(w_out, vec_out, 11))

    barrier = pltpu.get_barrier_semaphore()
    for step in (0, 1, -1):
        for date in (0, 1):
            here = has_col[step] if step else d != date

            @pl.when(here)
            def _():
                pl.semaphore_signal(
                    barrier,
                    inc=1,
                    device_id={"rows": r, "cols": c + step, "date": date},
                    device_id_type=MESH,
                )

            @pl.when(has_col[step] & has_other)
            def _():
                pl.semaphore_signal(
                    barrier,
                    inc=1,
                    device_id={"rows": other_row, "cols": c + step, "date": date},
                    device_id_type=MESH,
                )

    wl2[0:ch, ch:] = jnp.zeros((ch, ch), BF16)
    wl2[ch:, 0:ch] = jnp.zeros((ch, ch), BF16)
    for dst in (wf2, wd1, wd2):
        dst[depth:, 0:ch] = jnp.zeros((3 * ch, ch), BF16)
        dst[0 : 3 * ch, ch:] = jnp.zeros((3 * ch, ch), BF16)

    def start_row(date, place, kind):
        own = HALO[date] if place == 0 else 0
        other = 0 if place == 0 else half + HALO[date]
        return base_of[date] + (own if kind == 0 else other)

    for place in (0, 1):

        @pl.when((d == place) & jnp.logical_not(has_other))
        def _():
            for date in (0, 1):
                first = start_row(date, place, 1)
                field[first : first + HALO[date]] = jnp.zeros((HALO[date], groups, SIDE, ch), BF16)

    cols_beside = jnp.where(has_col[1], 1, 0) + jnp.where(has_col[-1], 1, 0) + 1
    rows_beside = jnp.where(has_down, 1, 0) + jnp.where(has_up, 1, 0)
    pl.semaphore_wait(barrier, (2 + rows_beside) * cols_beside - 1)

    def pieces(date):
        h = HALO[date]
        found = []
        for rk, (row_step, place, ok) in enumerate(
            (
                (0, 1 - date, None),
                (0, date, None),
                (1, 0, has_down),
                (-1, 1, has_up),
            )
        ):
            kind = 0 if row_step == 0 else 1
            count = half + h if kind == 0 else h
            if kind == 0:
                src_row = 0 if place == 0 else half - h
            else:
                src_row = tile_rows - h if place == 0 else 0
            dst_row = start_row(date, place, kind)
            for ck, step in enumerate((0, 1, -1)):
                if rk == 1 and step == 0:
                    continue
                src_col, dst_col, width = (
                    (0, 1, core),
                    (core - 1, 0, 1),
                    (0, 1 + core, 1),
                )[ck]
                go = has_col[step]
                if ok is not None:
                    go = go & ok
                copy = pltpu.make_async_remote_copy(
                    src_ref=feat.at[pl.ds(src_row, count), pl.ds(src_col, width)],
                    dst_ref=field.at[pl.ds(dst_row, count), pl.ds(dst_col, width)],
                    send_sem=send_sem.at[rk, ck],
                    recv_sem=recv_sem.at[date, kind, ck],
                    device_id={"rows": r + row_step, "cols": c + step, "date": place},
                    device_id_type=MESH,
                )
                found.append(((kind, -abs(step)), go, copy))
        found.sort(key=lambda item: item[0])
        return [item[1:] for item in found]

    def own_copy(date):
        h = HALO[date]
        return pltpu.make_async_copy(
            feat.at[pl.ds(0 if date == 0 else half - h, half + h)],
            field.at[pl.ds(start_row(date, date, 0), half + h), pl.ds(1, core)],
            recv_sem.at[date, 0, 0],
        )

    for date in (0, 1):

        @pl.when(d == date)
        def _():
            for go, copy in pieces(date):

                @pl.when(go)
                def _():
                    copy.start()

            own_copy(date).start()

    def await_kind(kind):
        for date in (0, 1):
            h = HALO[date]
            count = half + h if kind == 0 else h
            first = jnp.where(upper, start_row(date, 0, kind), start_row(date, 1, kind))
            for ck, step in enumerate((0, -1, 1)):
                dst_col, width = ((1, core), (0, 1), (1 + core, 1))[ck]
                view = field.at[pl.ds(first, count), pl.ds(dst_col, width)]

                def wait():
                    pltpu.make_async_copy(view, view, recv_sem.at[date, kind, ck]).wait()

                ok = has_col[step]
                if kind == 1:
                    ok = ok & has_other
                pl.when(ok)(wait)

    far = 1 << 20
    origin = (2 * r + d) * half
    rows_total = row_tiles * tile_rows
    left_end = -c * tile_cols
    right_end = (col_tiles - c) * tile_cols
    x_mid = lax.broadcasted_iota(jnp.int32, (mid, ch), 0) - SIDE
    edge = SIDE

    def inside(x, y):
        row = origin + y
        end = jnp.where((row >= 0) & (row < rows_total), right_end, -far)
        return (x >= left_end) & (x < end)

    def put_taps(dst, pair, slot, value, lo, hi):
        total = value.shape[0]
        at = slot * 3 * ch
        taps = (pltpu.roll(value, 1, 0), value, pltpu.roll(value, total - 1, 0))
        for tap, moved in enumerate(taps):
            dst[pair, :, at + tap * ch : at + (tap + 1) * ch] = moved[lo:hi].astype(BF16)

    def lateral_pair(date, q):
        first = base_of[date] + 2 * q
        both = jnp.concatenate(
            [field[first + slot].reshape(mid, ch) for slot in (0, 1)], axis=-1
        )
        value = jnp.dot(both, wl2[...], preferred_element_type=F32)
        for slot in (0, 1):
            y = 2 * q + slot - HALO[date]
            part = value[:, slot * ch : (slot + 1) * ch] + lat_bias
            part = jnp.where(inside(x_mid, y), part, 0.0)
            put_taps(lat6, base_of[date] // 2 + q, slot, part, 0, mid)

    def conv_pairs(src, weights, first, count):
        width, deep = src.shape[1:]
        top = src[pl.ds(first, count)].reshape(count * width, deep)
        low = src[pl.ds(first + 1, count)].reshape(count * width, deep)
        return jnp.dot(top, weights[0:deep], preferred_element_type=F32) + jnp.dot(
            low, weights[deep:], preferred_element_type=F32
        )

    def pyramid_pairs(date, q, count):
        value = conv_pairs(lat6, wf2, base_of[date] // 2 + q, count)
        value = value.astype(BF16).astype(F32)
        for pair in range(count):
            for slot in (0, 1):
                part = value[pair * mid : (pair + 1) * mid, slot * ch : (slot + 1) * ch]
                if date == 0:
                    pyr_a[2 * (q + pair) + slot] = part
                else:
                    pyr_b[2 * (q + pair) + slot, edge : edge + mid] = part

    def phase(kind):
        for date in (0, 1):
            pairs = rows_of[date] // 2
            late = (HALO[date] + 1) // 2
            count = pairs - late if kind == 0 else late
            low_first = 0 if kind == 0 else pairs - late
            first = jnp.where(upper, pairs - count - low_first, low_first)

            def body(i, carry):
                lateral_pair(date, first + i)
                return carry

            lax.fori_loop(0, count, body, 0, unroll=True)
        if kind == 0:
            for copy in conv_copies[0]:
                copy.wait()
        for date in (0, 1):
            pairs = rows_of[date] // 2 - 1
            late = (HALO[date] + 1) // 2
            count = pairs - late if kind == 0 else late
            low_first = 0 if kind == 0 else pairs - late
            first = jnp.where(upper, pairs - count - low_first, low_first)

            def body(i, carry):
                pyramid_pairs(date, first + 2 * i, 2)
                return carry

            pyramid_pairs(date, first, count)

    for copy in lat_copies:
        copy.wait()
    lat_bias = vec_lat[...]
    await_kind(0)
    phase(0)
    await_kind(1)
    phase(1)

    tiles = []
    for kind in (0, 1):
        tile_row = r if kind == 0 else jnp.clip(other_row, 0, row_tiles - 1)
        for step in (0, -1, 1):
            tile_col = jnp.clip(c + step, 0, col_tiles - 1)
            ok = has_col[step]
            if kind == 1:
                ok = ok & has_other
            tiles.append((kind, step, ok, shift_ref[tile_col, 0, tile_row], shift_ref[tile_col, 1, tile_row]))
    reach = HALO[1] - 1
    x_left = x_mid[0 : 2 * SIDE]
    x_right = x_mid[mid - 2 * SIDE : mid]

    def regrid_row(p, slot):
        y = 2 * p + slot - 2
        sums = {0: 0.0, -1: 0.0, 1: 0.0}
        seen = {0: 0.0, -1: 0.0, 1: 0.0}
        for kind, step, ok, row_by, col_by in tiles:
            u = y + d * half - row_by
            within = (u >= 0) & (u < tile_rows)
            use = ok & (within if kind == 0 else jnp.logical_not(within))
            if step == 0:
                x, start, size = x_mid, 0, mid
                low, high = col_by, tile_cols + col_by
            elif step == -1:
                x, start, size = x_left, 0, 2 * SIDE
                low, high = -far, col_by
            else:
                x, start, size = x_right, mid - 2 * SIDE, 2 * SIDE
                low, high = tile_cols + col_by, far
            mask = (x >= low) & (x < jnp.where(use, high, -2 * far))
            piece = pyr_b[y - row_by + reach, pl.ds(start + edge - col_by, size), :]
            sums[step] = sums[step] + jnp.where(mask, piece, 0.0)
            seen[step] = seen[step] + jnp.where(mask, 1.0, 0.0)

        def whole(parts):
            full = parts[0]
            return jnp.concatenate(
                [
                    full[0 : 2 * SIDE] + parts[-1],
                    full[2 * SIDE : mid - 2 * SIDE],
                    full[mid - 2 * SIDE :] + parts[1],
                ],
                axis=0,
            )

        total, cover = whole(sums), whole(seen)
        placed = total / jnp.maximum(cover, 1.0)
        diff = jnp.abs(pyr_a[2 * p + slot] - placed) * jnp.minimum(cover, 1.0)
        diff = jnp.where(inside(x_mid, y), diff, 0.0)
        put_taps(dif6, p, slot, diff, 0, mid)

    def regrid_body(p, carry):
        regrid_row(p, 0)
        regrid_row(p, 1)
        return carry

    lax.fori_loop(0, half // 2 + 2, regrid_body, 0)

    for copy in conv_copies[1]:
        copy.wait()
    bias_one = vec_one[...]

    def dec_one(i, count):
        value = conv_pairs(dif6, wd1, i, count)
        for pair in range(count):
            for slot in (0, 1):
                part = value[pair * mid : (pair + 1) * mid, slot * ch : (slot + 1) * ch]
                part = jnp.maximum(part + bias_one, 0.0)
                part = jnp.where(inside(x_mid, 2 * (i + pair) + slot - 1), part, 0.0)
                put_taps(hid6, i + pair, slot, part, edge, mid - edge)

    dec_one(0, half // 2 + 1)

    for copy in conv_copies[2]:
        copy.wait()
    bias_two = vec_two[...]
    out_w = jnp.broadcast_to(vec_out[...].astype(F32), (16, ch)).astype(BF16)
    out_b = b_out[0]
    for i in range(0, half // 2, half // 2):
        value = conv_pairs(hid6, wd2, i, half // 2)
        for pair in range(half // 2):
            for slot in (0, 1):
                part = value[pair * tile_cols : (pair + 1) * tile_cols, slot * ch : (slot + 1) * ch]
                part = jnp.maximum(part + bias_two, 0.0).astype(BF16)
                logit = lax.dot_general(
                    out_w, part, (((1,), (1,)), ((), ())), preferred_element_type=F32
                )
                y = 2 * (i + pair) + slot
                out_ref[y : y + 1, :] = logit[0:1] + out_b

    for date in (0, 1):

        @pl.when(d == date)
        def _():
            for go, copy in pieces(date):

                @pl.when(go)
                def _():
                    copy.wait_send()


def per_device(
    features, scene_shift, w_lat, b_lat, w_fpn, w_dec1, b_dec1, w_dec2, b_dec2, w_out, b_out
):
    tile_rows, tile_cols, ch = features.shape[1:]
    half = tile_rows // 2
    sizes = (lax.axis_size("rows"), lax.axis_size("cols"), tile_rows, tile_cols)
    rows_of = tuple(half + 2 * h for h in HALO)
    mid = tile_cols + 2 * SIDE
    hbm = pl.BlockSpec(memory_space=pltpu.HBM)
    vmem = pl.BlockSpec(memory_space=pltpu.VMEM)
    smem = pl.BlockSpec(memory_space=pltpu.SMEM)
    flops = 2 * ch * ch * tile_cols * 9 * 60
    return pl.pallas_call(
        functools.partial(kernel, sizes),
        out_shape=jax.ShapeDtypeStruct((half, tile_cols), F32),
        in_specs=[
            hbm,
            smem,
            hbm,
            hbm,
            hbm,
            hbm,
            hbm,
            hbm,
            hbm,
            hbm,
            smem,
        ],
        out_specs=vmem,
        scratch_shapes=[
            pltpu.VMEM((sum(rows_of), mid // SIDE, SIDE, ch), BF16),
            pltpu.VMEM((sum(rows_of) // 2, mid, 6 * ch), BF16),
            pltpu.VMEM((half + 4, mid, ch), F32),
            pltpu.VMEM((half + 2 * HALO[1] - 2, mid + 2 * SIDE, ch), F32),
            pltpu.VMEM((half // 2 + 2, mid, 6 * ch), BF16),
            pltpu.VMEM((half // 2 + 1, tile_cols, 6 * ch), BF16),
            pltpu.VMEM((2 * ch, 2 * ch), BF16),
            pltpu.VMEM((12 * ch, 2 * ch), BF16),
            pltpu.VMEM((12 * ch, 2 * ch), BF16),
            pltpu.VMEM((12 * ch, 2 * ch), BF16),
            pltpu.VMEM((1, ch), F32),
            pltpu.VMEM((1, ch), F32),
            pltpu.VMEM((1, ch), F32),
            pltpu.VMEM((1, ch), BF16),
            pltpu.SemaphoreType.DMA((4, 3)),
            pltpu.SemaphoreType.DMA((2, 2, 3)),
            pltpu.SemaphoreType.DMA((12,)),
        ],
        compiler_params=pltpu.CompilerParams(
            collective_id=0, has_side_effects=True, vmem_limit_bytes=60 << 20
        ),
        cost_estimate=pl.CostEstimate(flops=flops, bytes_accessed=4 << 20, transcendentals=0),
    )(
        features.reshape(tile_rows, tile_cols // SIDE, SIDE, ch),
        scene_shift.transpose(1, 2, 0),
        w_lat,
        b_lat.reshape(1, ch),
        w_fpn.reshape(9 * ch, ch),
        w_dec1.reshape(9 * ch, ch),
        b_dec1.reshape(1, ch),
        w_dec2.reshape(9 * ch, ch),
        b_dec2.reshape(1, ch),
        w_out.reshape(1, ch),
        b_out,
    )


def solution(mesh):
    return jax.shard_map(
        per_device,
        mesh=mesh,
        in_specs=(
            P("date", ("groups", "rows"), "cols", None),
            P("groups", None, None),
            P(),
            P(),
            P(),
            P(),
            P(),
            P(),
            P(),
            P(),
            P(),
        ),
        out_specs=P(("groups", "rows", "date"), "cols"),
        check_vma=False,
    )
```

```python
import functools

import jax
import jax.numpy as jnp
from jax import lax
from jax.experimental import pallas as pl
from jax.experimental.pallas import tpu as pltpu
from jax.sharding import PartitionSpec as P

MO = 4
HALO = (3, 2 + MO + 1)
SIDE = 8
MESH = pl.DeviceIdType.MESH
F32 = jnp.float32
BF16 = jnp.bfloat16


def kernel(
    sizes,
    feat,
    shift_ref,
    w_lat,
    b_lat,
    w_fpn,
    w_dec1,
    b_dec1,
    w_dec2,
    b_dec2,
    w_out,
    b_out,
    out_ref,
    field,
    lat6,
    pyr_a,
    pyr_b,
    dif6,
    hid6,
    wl2,
    wf2,
    wd1,
    wd2,
    vec_lat,
    vec_one,
    vec_two,
    vec_out,
    send_sem,
    recv_sem,
    copy_sem,
):
    row_tiles, col_tiles, tile_rows, tile_cols = sizes
    half = tile_rows // 2
    mid = tile_cols + 2 * SIDE
    groups = mid // SIDE
    core = tile_cols // SIDE
    rows_of = tuple(half + 2 * h for h in HALO)
    base_of = (0, rows_of[0])
    ch = feat.shape[3]
    r = lax.axis_index("rows")
    c = lax.axis_index("cols")
    d = lax.axis_index("date")
    upper = d == 0
    has_col = {0: c >= 0, 1: c + 1 < col_tiles, -1: c >= 1}
    has_down = r + 1 < row_tiles
    has_up = r >= 1
    other_row = jnp.where(upper, r - 1, r + 1)
    has_other = (other_row >= 0) & (other_row < row_tiles)

    def local(src, dst, index):
        copy = pltpu.make_async_copy(src, dst, copy_sem.at[index])
        copy.start()
        return copy

    depth = 9 * ch
    lat_copies = [
        local(w_lat, wl2.at[pl.ds(0, ch), pl.ds(0, ch)], 0),
        local(w_lat, wl2.at[pl.ds(ch, ch), pl.ds(ch, ch)], 1),
    ]
    lat_copies.append(local(b_lat, vec_lat, 8))
    conv_copies = []
    for at, (src, dst) in enumerate(((w_fpn, wf2), (w_dec1, wd1), (w_dec2, wd2))):
        conv_copies.append(
            [
                local(src, dst.at[pl.ds(0, depth), pl.ds(0, ch)], 2 + 2 * at),
                local(src, dst.at[pl.ds(3 * ch, depth), pl.ds(ch, ch)], 3 + 2 * at),
            ]
        )
    conv_copies[1].append(local(b_dec1, vec_one, 9))
    conv_copies[2].append(local(b_dec2, vec_two, 10))
    conv_copies[2].append(local(w_out, vec_out, 11))

    def start_row(date, place, kind):
        own = HALO[date] if place == 0 else 0
        other = 0 if place == 0 else half + HALO[date]
        return base_of[date] + (own if kind == 0 else other)

    def own_copy(date):
        h = HALO[date]
        return pltpu.make_async_copy(
            feat.at[pl.ds(0 if date == 0 else half - h, half + h)],
            field.at[pl.ds(start_row(date, date, 0), half + h), pl.ds(1, core)],
            recv_sem.at[date, 0, 0],
        )

    for date in (0, 1):

        @pl.when(d == date)
        def _():
            own_copy(date).start()

    barrier = pltpu.get_barrier_semaphore()
    for step in (0, 1, -1):
        for date in (0, 1):
            here = has_col[step] if step else d != date

            @pl.when(here)
            def _():
                pl.semaphore_signal(
                    barrier,
                    inc=1,
                    device_id={"rows": r, "cols": c + step, "date": date},
                    device_id_type=MESH,
                )

            @pl.when(has_col[step] & has_other)
            def _():
                pl.semaphore_signal(
                    barrier,
                    inc=1,
                    device_id={"rows": other_row, "cols": c + step, "date": date},
                    device_id_type=MESH,
                )

    wl2[0:ch, ch:] = jnp.zeros((ch, ch), BF16)
    wl2[ch:, 0:ch] = jnp.zeros((ch, ch), BF16)
    for dst in (wf2, wd1, wd2):
        dst[depth:, 0:ch] = jnp.zeros((3 * ch, ch), BF16)
        dst[0 : 3 * ch, ch:] = jnp.zeros((3 * ch, ch), BF16)

    for place in (0, 1):

        @pl.when((d == place) & jnp.logical_not(has_other))
        def _():
            for date in (0, 1):
                first = start_row(date, place, 1)
                field[first : first + HALO[date]] = jnp.zeros((HALO[date], groups, SIDE, ch), BF16)

    cols_beside = jnp.where(has_col[1], 1, 0) + jnp.where(has_col[-1], 1, 0) + 1
    rows_beside = jnp.where(has_down, 1, 0) + jnp.where(has_up, 1, 0)
    pl.semaphore_wait(barrier, (2 + rows_beside) * cols_beside - 1)

    def pieces(date):
        h = HALO[date]
        found = []
        for rk, (row_step, place, ok) in enumerate(
            (
                (0, 1 - date, None),
                (0, date, None),
                (1, 0, has_down),
                (-1, 1, has_up),
            )
        ):
            kind = 0 if row_step == 0 else 1
            count = half + h if kind == 0 else h
            if kind == 0:
                src_row = 0 if place == 0 else half - h
            else:
                src_row = tile_rows - h if place == 0 else 0
            dst_row = start_row(date, place, kind)
            for ck, step in enumerate((0, 1, -1)):
                if rk == 1 and step == 0:
                    continue
                src_col, dst_col, width = (
                    (0, 1, core),
                    (core - 1, 0, 1),
                    (0, 1 + core, 1),
                )[ck]
                go = has_col[step]
                if ok is not None:
                    go = go & ok
                copy = pltpu.make_async_remote_copy(
                    src_ref=feat.at[pl.ds(src_row, count), pl.ds(src_col, width)],
                    dst_ref=field.at[pl.ds(dst_row, count), pl.ds(dst_col, width)],
                    send_sem=send_sem.at[rk, ck],
                    recv_sem=recv_sem.at[date, kind, ck],
                    device_id={"rows": r + row_step, "cols": c + step, "date": place},
                    device_id_type=MESH,
                )
                late = {(1, 0): 0, (0, 1): 1, (0, 0): 2, (1, 1): 3}[kind, abs(step)]
                found.append((late, go, copy))
        found.sort(key=lambda item: item[0])
        return [item[1:] for item in found]

    for date in (0, 1):

        @pl.when(d == date)
        def _():
            for go, copy in pieces(date):

                @pl.when(go)
                def _():
                    copy.start()

    def await_kind(kind, steps=(0, -1, 1), dates=(0, 1)):
        for date in dates:
            h = HALO[date]
            count = half + h if kind == 0 else h
            first = jnp.where(upper, start_row(date, 0, kind), start_row(date, 1, kind))
            for ck, step in enumerate((0, -1, 1)):
                dst_col, width = ((1, core), (0, 1), (1 + core, 1))[ck]
                if step not in steps:
                    continue
                view = field.at[pl.ds(first, count), pl.ds(dst_col, width)]

                def wait():
                    pltpu.make_async_copy(view, view, recv_sem.at[date, kind, ck]).wait()

                ok = has_col[step]
                if kind == 1:
                    ok = ok & has_other
                pl.when(ok)(wait)

    far = 1 << 20
    origin = (2 * r + d) * half
    rows_total = row_tiles * tile_rows
    left_end = -c * tile_cols
    right_end = (col_tiles - c) * tile_cols
    x_mid = lax.broadcasted_iota(jnp.int32, (mid, ch), 0) - SIDE
    edge = SIDE

    def inside(x, y):
        row = origin + y
        end = jnp.where((row >= 0) & (row < rows_total), right_end, -far)
        return (x >= left_end) & (x < end)

    def put_taps(dst, pair, slot, value, lo, hi):
        total = value.shape[0]
        at = slot * 3 * ch
        taps = (pltpu.roll(value, 1, 0), value, pltpu.roll(value, total - 1, 0))
        for tap, moved in enumerate(taps):
            dst[pair, :, at + tap * ch : at + (tap + 1) * ch] = moved[lo:hi].astype(BF16)

    def lateral_pair(date, q):
        first = base_of[date] + 2 * q
        both = jnp.concatenate(
            [field[first + slot].reshape(mid, ch) for slot in (0, 1)], axis=-1
        )
        value = jnp.dot(both, wl2[...], preferred_element_type=F32)
        for slot in (0, 1):
            y = 2 * q + slot - HALO[date]
            part = value[:, slot * ch : (slot + 1) * ch] + lat_bias
            part = jnp.where(inside(x_mid, y), part, 0.0)
            put_taps(lat6, base_of[date] // 2 + q, slot, part, 0, mid)

    def pairs_first(date):
        return jnp.where(upper, (HALO[date] + 1) // 2, 0)

    def pairs_count(date):
        return rows_of[date] // 2 - (HALO[date] + 1) // 2

    def lateral_core(date):
        none = jnp.zeros((SIDE, ch), F32)
        for i in range(pairs_count(date)):
            q = pairs_first(date) + i
            first = base_of[date] + 2 * q
            both = jnp.concatenate(
                [field[first + slot, 1 : 1 + core].reshape(tile_cols, ch) for slot in (0, 1)],
                axis=-1,
            )
            value = jnp.dot(both, wl2[...], preferred_element_type=F32)
            for slot in (0, 1):
                part = value[:, slot * ch : (slot + 1) * ch] + lat_bias
                part = jnp.concatenate([none, part, none], axis=0)
                put_taps(lat6, base_of[date] // 2 + q, slot, part, 0, mid)

    def lateral_sides(date):
        rows = 2 * pairs_count(date)
        q = pairs_first(date)
        strip = 3 * SIDE
        for at, shift in ((0, 0), (groups - 3, SIDE)):
            block = field[pl.ds(base_of[date] + 2 * q, rows), at : at + 3]
            value = jnp.dot(
                block.reshape(rows * strip, ch), wl2[0:ch, 0:ch], preferred_element_type=F32
            )
            x = lax.broadcasted_iota(jnp.int32, (rows, strip, ch), 1) + (at - 1) * SIDE
            x = x.reshape(rows * strip, ch)
            value = jnp.where((x >= left_end) & (x < right_end), value + lat_bias, 0.0)
            taps = (pltpu.roll(value, 1, 0), value, pltpu.roll(value, rows * strip - 1, 0))
            low = at * SIDE + shift
            for i in range(rows):
                pair = base_of[date] // 2 + q + i // 2
                for tap, moved in enumerate(taps):
                    lane = (i % 2) * 3 * ch + tap * ch
                    part = moved[i * strip + shift : i * strip + shift + 2 * SIDE]
                    lat6[pair, low : low + 2 * SIDE, lane : lane + ch] = part.astype(BF16)

    def conv_pairs(src, weights, first, count):
        width, deep = src.shape[1:]
        top = src[pl.ds(first, count)].reshape(count * width, deep)
        low = src[pl.ds(first + 1, count)].reshape(count * width, deep)
        return jnp.dot(top, weights[0:deep], preferred_element_type=F32) + jnp.dot(
            low, weights[deep:], preferred_element_type=F32
        )

    def pyramid_pairs(date, q, count):
        value = conv_pairs(lat6, wf2, base_of[date] // 2 + q, count)
        value = value.astype(BF16).astype(F32)
        for pair in range(count):
            for slot in (0, 1):
                part = value[pair * mid : (pair + 1) * mid, slot * ch : (slot + 1) * ch]
                if date == 0:
                    pyr_a[2 * (q + pair) + slot] = part
                else:
                    pyr_b[2 * (q + pair) + slot, edge : edge + mid] = part

    def phase(kind):
        for date in (0, 1) if kind == 1 else ():
            pairs = rows_of[date] // 2
            late = (HALO[date] + 1) // 2
            count = pairs - late if kind == 0 else late
            low_first = 0 if kind == 0 else pairs - late
            first = jnp.where(upper, pairs - count - low_first, low_first)

            def body(i, carry):
                lateral_pair(date, first + i)
                return carry

            lax.fori_loop(0, count, body, 0, unroll=True)
        if kind == 0:
            for copy in conv_copies[0]:
                copy.wait()
        for date in (0, 1):
            pairs = rows_of[date] // 2 - 1
            late = (HALO[date] + 1) // 2
            count = pairs - late if kind == 0 else late
            low_first = 0 if kind == 0 else pairs - late
            first = jnp.where(upper, pairs - count - low_first, low_first)

            def body(i, carry):
                pyramid_pairs(date, first + 2 * i, 2)
                return carry

            pyramid_pairs(date, first, count)

    for copy in lat_copies:
        copy.wait()
    lat_bias = vec_lat[...]
    for date in (0, 1):

        @pl.when(d == date)
        def _():
            own_copy(date).wait()
            lateral_core(date)

    for date in (0, 1):

        @pl.when(d != date)
        def _():
            await_kind(0, (0,), (date,))
            lateral_core(date)

    await_kind(0, (-1, 1))
    for date in (0, 1):
        lateral_sides(date)
    phase(0)
    await_kind(1)
    phase(1)

    tiles = []
    for kind in (0, 1):
        tile_row = r if kind == 0 else jnp.clip(other_row, 0, row_tiles - 1)
        for step in (0, -1, 1):
            tile_col = jnp.clip(c + step, 0, col_tiles - 1)
            ok = has_col[step]
            if kind == 1:
                ok = ok & has_other
            tiles.append((kind, step, ok, shift_ref[tile_col, 0, tile_row], shift_ref[tile_col, 1, tile_row]))
    reach = HALO[1] - 1
    x_left = x_mid[0 : 2 * SIDE]
    x_right = x_mid[mid - 2 * SIDE : mid]

    def regrid_row(p, slot):
        y = 2 * p + slot - 2
        sums = {0: 0.0, -1: 0.0, 1: 0.0}
        seen = {0: 0.0, -1: 0.0, 1: 0.0}
        for kind, step, ok, row_by, col_by in tiles:
            u = y + d * half - row_by
            within = (u >= 0) & (u < tile_rows)
            use = ok & (within if kind == 0 else jnp.logical_not(within))
            if step == 0:
                x, start, size = x_mid, 0, mid
                low, high = col_by, tile_cols + col_by
            elif step == -1:
                x, start, size = x_left, 0, 2 * SIDE
                low, high = -far, col_by
            else:
                x, start, size = x_right, mid - 2 * SIDE, 2 * SIDE
                low, high = tile_cols + col_by, far
            mask = (x >= low) & (x < jnp.where(use, high, -2 * far))
            piece = pyr_b[y - row_by + reach, pl.ds(start + edge - col_by, size), :]
            sums[step] = sums[step] + jnp.where(mask, piece, 0.0)
            seen[step] = seen[step] + jnp.where(mask, 1.0, 0.0)

        def whole(parts):
            full = parts[0]
            return jnp.concatenate(
                [
                    full[0 : 2 * SIDE] + parts[-1],
                    full[2 * SIDE : mid - 2 * SIDE],
                    full[mid - 2 * SIDE :] + parts[1],
                ],
                axis=0,
            )

        total, cover = whole(sums), whole(seen)
        placed = total / jnp.maximum(cover, 1.0)
        diff = jnp.abs(pyr_a[2 * p + slot] - placed) * jnp.minimum(cover, 1.0)
        diff = jnp.where(inside(x_mid, y), diff, 0.0)
        put_taps(dif6, p, slot, diff, 0, mid)

    def regrid_body(p, carry):
        regrid_row(p, 0)
        regrid_row(p, 1)
        return carry

    lax.fori_loop(0, half // 2 + 2, regrid_body, 0)

    for copy in conv_copies[1]:
        copy.wait()
    bias_one = vec_one[...]

    def dec_one(i, count):
        value = conv_pairs(dif6, wd1, i, count)
        for pair in range(count):
            for slot in (0, 1):
                part = value[pair * mid : (pair + 1) * mid, slot * ch : (slot + 1) * ch]
                part = jnp.maximum(part + bias_one, 0.0)
                part = jnp.where(inside(x_mid, 2 * (i + pair) + slot - 1), part, 0.0)
                put_taps(hid6, i + pair, slot, part, edge, mid - edge)

    dec_one(0, half // 2 + 1)

    for copy in conv_copies[2]:
        copy.wait()
    bias_two = vec_two[...]
    out_w = jnp.broadcast_to(vec_out[...].astype(F32), (16, ch)).astype(BF16)
    out_b = b_out[0]
    for i in range(0, half // 2, half // 2):
        value = conv_pairs(hid6, wd2, i, half // 2)
        for pair in range(half // 2):
            for slot in (0, 1):
                part = value[pair * tile_cols : (pair + 1) * tile_cols, slot * ch : (slot + 1) * ch]
                part = jnp.maximum(part + bias_two, 0.0).astype(BF16)
                logit = lax.dot_general(
                    out_w, part, (((1,), (1,)), ((), ())), preferred_element_type=F32
                )
                y = 2 * (i + pair) + slot
                out_ref[y : y + 1, :] = logit[0:1] + out_b

    for date in (0, 1):

        @pl.when(d == date)
        def _():
            for go, copy in pieces(date):

                @pl.when(go)
                def _():
                    copy.wait_send()


def per_device(
    features, scene_shift, w_lat, b_lat, w_fpn, w_dec1, b_dec1, w_dec2, b_dec2, w_out, b_out
):
    tile_rows, tile_cols, ch = features.shape[1:]
    half = tile_rows // 2
    sizes = (lax.axis_size("rows"), lax.axis_size("cols"), tile_rows, tile_cols)
    rows_of = tuple(half + 2 * h for h in HALO)
    mid = tile_cols + 2 * SIDE
    hbm = pl.BlockSpec(memory_space=pltpu.HBM)
    vmem = pl.BlockSpec(memory_space=pltpu.VMEM)
    smem = pl.BlockSpec(memory_space=pltpu.SMEM)
    flops = 2 * ch * ch * tile_cols * 9 * 60
    return pl.pallas_call(
        functools.partial(kernel, sizes),
        out_shape=pltpu.VMEM((half, tile_cols), F32),
        in_specs=[
            hbm,
            smem,
            hbm,
            hbm,
            hbm,
            hbm,
            hbm,
            hbm,
            hbm,
            hbm,
            smem,
        ],
        out_specs=vmem,
        scratch_shapes=[
            pltpu.VMEM((sum(rows_of), mid // SIDE, SIDE, ch), BF16),
            pltpu.VMEM((sum(rows_of) // 2, mid, 6 * ch), BF16),
            pltpu.VMEM((half + 4, mid, ch), F32),
            pltpu.VMEM((half + 2 * HALO[1] - 2, mid + 2 * SIDE, ch), F32),
            pltpu.VMEM((half // 2 + 2, mid, 6 * ch), BF16),
            pltpu.VMEM((half // 2 + 1, tile_cols, 6 * ch), BF16),
            pltpu.VMEM((2 * ch, 2 * ch), BF16),
            pltpu.VMEM((12 * ch, 2 * ch), BF16),
            pltpu.VMEM((12 * ch, 2 * ch), BF16),
            pltpu.VMEM((12 * ch, 2 * ch), BF16),
            pltpu.VMEM((1, ch), F32),
            pltpu.VMEM((1, ch), F32),
            pltpu.VMEM((1, ch), F32),
            pltpu.VMEM((1, ch), BF16),
            pltpu.SemaphoreType.DMA((4, 3)),
            pltpu.SemaphoreType.DMA((2, 2, 3)),
            pltpu.SemaphoreType.DMA((12,)),
        ],
        compiler_params=pltpu.CompilerParams(
            collective_id=0, has_side_effects=True, vmem_limit_bytes=60 << 20
        ),
        cost_estimate=pl.CostEstimate(flops=flops, bytes_accessed=4 << 20, transcendentals=0),
    )(
        features.reshape(tile_rows, tile_cols // SIDE, SIDE, ch),
        scene_shift.transpose(1, 2, 0),
        w_lat,
        b_lat.reshape(1, ch),
        w_fpn.reshape(9 * ch, ch),
        w_dec1.reshape(9 * ch, ch),
        b_dec1.reshape(1, ch),
        w_dec2.reshape(9 * ch, ch),
        b_dec2.reshape(1, ch),
        w_out.reshape(1, ch),
        b_out,
    )


def solution(mesh):
    return jax.shard_map(
        per_device,
        mesh=mesh,
        in_specs=(
            P("date", ("groups", "rows"), "cols", None),
            P("groups", None, None),
            P(),
            P(),
            P(),
            P(),
            P(),
            P(),
            P(),
            P(),
            P(),
        ),
        out_specs=P(("groups", "rows", "date"), "cols"),
        check_vma=False,
    )
```

```python
import functools

import jax
import jax.numpy as jnp
from jax import lax
from jax.experimental import pallas as pl
from jax.experimental.pallas import tpu as pltpu
from jax.sharding import PartitionSpec as P

MO = 4
HALO = (3, 2 + MO + 1)
SIDE = 8
MESH = pl.DeviceIdType.MESH
F32 = jnp.float32
BF16 = jnp.bfloat16


def kernel(
    sizes,
    feat,
    shift_ref,
    w_lat,
    b_lat,
    w_fpn,
    w_dec1,
    b_dec1,
    w_dec2,
    b_dec2,
    w_out,
    b_out,
    out_ref,
    field,
    lat6,
    pyr_a,
    pyr_b,
    dif6,
    hid6,
    wl2,
    wf2,
    wd1,
    wd2,
    vec_lat,
    vec_one,
    vec_two,
    vec_out,
    send_sem,
    recv_sem,
    copy_sem,
):
    row_tiles, col_tiles, tile_rows, tile_cols = sizes
    half = tile_rows // 2
    mid = tile_cols + 2 * SIDE
    groups = mid // SIDE
    core = tile_cols // SIDE
    rows_of = tuple(half + 2 * h for h in HALO)
    base_of = (0, rows_of[0])
    ch = feat.shape[3]
    r = lax.axis_index("rows")
    c = lax.axis_index("cols")
    d = lax.axis_index("date")
    upper = d == 0
    has_col = {0: c >= 0, 1: c + 1 < col_tiles, -1: c >= 1}
    has_down = r + 1 < row_tiles
    has_up = r >= 1
    other_row = jnp.where(upper, r - 1, r + 1)
    has_other = (other_row >= 0) & (other_row < row_tiles)

    def local(src, dst, index):
        copy = pltpu.make_async_copy(src, dst, copy_sem.at[index])
        copy.start()
        return copy

    depth = 9 * ch
    lat_copies = [
        local(w_lat, wl2.at[pl.ds(0, ch), pl.ds(0, ch)], 0),
        local(w_lat, wl2.at[pl.ds(ch, ch), pl.ds(ch, ch)], 1),
    ]
    lat_copies.append(local(b_lat, vec_lat, 8))
    conv_copies = []
    for at, (src, dst) in enumerate(((w_fpn, wf2), (w_dec1, wd1), (w_dec2, wd2))):
        conv_copies.append(
            [
                local(src, dst.at[pl.ds(0, depth), pl.ds(0, ch)], 2 + 2 * at),
                local(src, dst.at[pl.ds(3 * ch, depth), pl.ds(ch, ch)], 3 + 2 * at),
            ]
        )
    conv_copies[1].append(local(b_dec1, vec_one, 9))
    conv_copies[2].append(local(b_dec2, vec_two, 10))
    conv_copies[2].append(local(w_out, vec_out, 11))

    def start_row(date, place, kind):
        own = HALO[date] if place == 0 else 0
        other = 0 if place == 0 else half + HALO[date]
        return base_of[date] + (own if kind == 0 else other)

    def own_copy(date):
        h = HALO[date]
        return pltpu.make_async_copy(
            feat.at[pl.ds(0 if date == 0 else half - h, half + h)],
            field.at[pl.ds(start_row(date, date, 0), half + h), pl.ds(1, core)],
            recv_sem.at[date, 0, 0],
        )

    for date in (0, 1):

        @pl.when(d == date)
        def _():
            own_copy(date).start()

    barrier = pltpu.get_barrier_semaphore()
    for step in (0, 1, -1):
        for date in (0, 1):
            here = has_col[step] if step else d != date

            @pl.when(here)
            def _():
                pl.semaphore_signal(
                    barrier,
                    inc=1,
                    device_id={"rows": r, "cols": c + step, "date": date},
                    device_id_type=MESH,
                )

            @pl.when(has_col[step] & has_other)
            def _():
                pl.semaphore_signal(
                    barrier,
                    inc=1,
                    device_id={"rows": other_row, "cols": c + step, "date": date},
                    device_id_type=MESH,
                )

    wl2[0:ch, ch:] = jnp.zeros((ch, ch), BF16)
    wl2[ch:, 0:ch] = jnp.zeros((ch, ch), BF16)
    for dst in (wf2, wd1, wd2):
        dst[depth:, 0:ch] = jnp.zeros((3 * ch, ch), BF16)
        dst[0 : 3 * ch, ch:] = jnp.zeros((3 * ch, ch), BF16)

    for place in (0, 1):

        @pl.when((d == place) & jnp.logical_not(has_other))
        def _():
            for date in (0, 1):
                first = start_row(date, place, 1)
                field[first : first + HALO[date]] = jnp.zeros((HALO[date], groups, SIDE, ch), BF16)

    cols_beside = jnp.where(has_col[1], 1, 0) + jnp.where(has_col[-1], 1, 0) + 1
    rows_beside = jnp.where(has_down, 1, 0) + jnp.where(has_up, 1, 0)
    pl.semaphore_wait(barrier, (2 + rows_beside) * cols_beside - 1)

    def pieces(date):
        h = HALO[date]
        found = []
        for rk, (row_step, place, ok) in enumerate(
            (
                (0, 1 - date, None),
                (0, date, None),
                (1, 0, has_down),
                (-1, 1, has_up),
            )
        ):
            kind = 0 if row_step == 0 else 1
            count = half + h if kind == 0 else h
            if kind == 0:
                src_row = 0 if place == 0 else half - h
            else:
                src_row = tile_rows - h if place == 0 else 0
            dst_row = start_row(date, place, kind)
            for ck, step in enumerate((0, 1, -1)):
                if rk == 1 and step == 0:
                    continue
                src_col, dst_col, width = (
                    (0, 1, core),
                    (core - 1, 0, 1),
                    (0, 1 + core, 1),
                )[ck]
                go = has_col[step]
                if ok is not None:
                    go = go & ok
                copy = pltpu.make_async_remote_copy(
                    src_ref=feat.at[pl.ds(src_row, count), pl.ds(src_col, width)],
                    dst_ref=field.at[pl.ds(dst_row, count), pl.ds(dst_col, width)],
                    send_sem=send_sem.at[rk, ck],
                    recv_sem=recv_sem.at[date, kind, ck],
                    device_id={"rows": r + row_step, "cols": c + step, "date": place},
                    device_id_type=MESH,
                )
                late = {(1, 0): 0, (0, 1): 1, (0, 0): 2, (1, 1): 3}[kind, abs(step)]
                found.append((late, go, copy))
        found.sort(key=lambda item: item[0])
        return [item[1:] for item in found]

    for date in (0, 1):

        @pl.when(d == date)
        def _():
            for go, copy in pieces(date):

                @pl.when(go)
                def _():
                    copy.start()

    def await_kind(kind, steps=(0, -1, 1), dates=(0, 1)):
        for date in dates:
            h = HALO[date]
            count = half + h if kind == 0 else h
            first = jnp.where(upper, start_row(date, 0, kind), start_row(date, 1, kind))
            for ck, step in enumerate((0, -1, 1)):
                dst_col, width = ((1, core), (0, 1), (1 + core, 1))[ck]
                if step not in steps:
                    continue
                view = field.at[pl.ds(first, count), pl.ds(dst_col, width)]

                def wait():
                    pltpu.make_async_copy(view, view, recv_sem.at[date, kind, ck]).wait()

                ok = has_col[step]
                if kind == 1:
                    ok = ok & has_other
                pl.when(ok)(wait)

    far = 1 << 20
    origin = (2 * r + d) * half
    rows_total = row_tiles * tile_rows
    left_end = -c * tile_cols
    right_end = (col_tiles - c) * tile_cols
    x_mid = lax.broadcasted_iota(jnp.int32, (mid, ch), 0) - SIDE
    edge = SIDE

    def inside(x, y):
        row = origin + y
        end = jnp.where((row >= 0) & (row < rows_total), right_end, -far)
        return (x >= left_end) & (x < end)

    def put_taps(dst, pair, slot, value, lo, hi):
        total = value.shape[0]
        at = slot * 3 * ch
        taps = (pltpu.roll(value, 1, 0), value, pltpu.roll(value, total - 1, 0))
        for tap, moved in enumerate(taps):
            dst[pair, :, at + tap * ch : at + (tap + 1) * ch] = moved[lo:hi].astype(BF16)

    def lateral_pair(date, q):
        first = base_of[date] + 2 * q
        both = jnp.concatenate(
            [field[first + slot].reshape(mid, ch) for slot in (0, 1)], axis=-1
        )
        value = jnp.dot(both, wl2[...], preferred_element_type=F32)
        for slot in (0, 1):
            y = 2 * q + slot - HALO[date]
            part = value[:, slot * ch : (slot + 1) * ch] + lat_bias
            part = jnp.where(inside(x_mid, y), part, 0.0)
            put_taps(lat6, base_of[date] // 2 + q, slot, part, 0, mid)

    def pairs_first(date):
        return jnp.where(upper, (HALO[date] + 1) // 2, 0)

    def pairs_count(date):
        return rows_of[date] // 2 - (HALO[date] + 1) // 2

    def lateral_core(date):
        none = jnp.zeros((SIDE, ch), F32)
        for i in range(pairs_count(date)):
            q = pairs_first(date) + i
            first = base_of[date] + 2 * q
            both = jnp.concatenate(
                [field[first + slot, 1 : 1 + core].reshape(tile_cols, ch) for slot in (0, 1)],
                axis=-1,
            )
            value = jnp.dot(both, wl2[...], preferred_element_type=F32)
            for slot in (0, 1):
                part = value[:, slot * ch : (slot + 1) * ch] + lat_bias
                part = jnp.concatenate([none, part, none], axis=0)
                put_taps(lat6, base_of[date] // 2 + q, slot, part, 0, mid)

    def lateral_sides(date):
        rows = 2 * pairs_count(date)
        q = pairs_first(date)
        strip = 3 * SIDE
        for at, shift in ((0, 0), (groups - 3, SIDE)):
            block = field[pl.ds(base_of[date] + 2 * q, rows), at : at + 3]
            value = jnp.dot(
                block.reshape(rows * strip, ch), wl2[0:ch, 0:ch], preferred_element_type=F32
            )
            x = lax.broadcasted_iota(jnp.int32, (rows, strip, ch), 1) + (at - 1) * SIDE
            x = x.reshape(rows * strip, ch)
            value = jnp.where((x >= left_end) & (x < right_end), value + lat_bias, 0.0)
            taps = (pltpu.roll(value, 1, 0), value, pltpu.roll(value, rows * strip - 1, 0))
            low = at * SIDE + shift
            for i in range(rows):
                pair = base_of[date] // 2 + q + i // 2
                for tap, moved in enumerate(taps):
                    lane = (i % 2) * 3 * ch + tap * ch
                    part = moved[i * strip + shift : i * strip + shift + 2 * SIDE]
                    lat6[pair, low : low + 2 * SIDE, lane : lane + ch] = part.astype(BF16)

    def conv_pairs(src, weights, first, count):
        width, deep = src.shape[1:]
        top = src[pl.ds(first, count)].reshape(count * width, deep)
        low = src[pl.ds(first + 1, count)].reshape(count * width, deep)
        return jnp.dot(top, weights[0:deep], preferred_element_type=F32) + jnp.dot(
            low, weights[deep:], preferred_element_type=F32
        )

    def pyramid_pairs(date, q, count):
        value = conv_pairs(lat6, wf2, base_of[date] // 2 + q, count)
        value = value.astype(BF16).astype(F32)
        for pair in range(count):
            for slot in (0, 1):
                part = value[pair * mid : (pair + 1) * mid, slot * ch : (slot + 1) * ch]
                if date == 0:
                    pyr_a[2 * (q + pair) + slot] = part
                else:
                    pyr_b[2 * (q + pair) + slot, edge : edge + mid] = part

    def phase(kind):
        for date in (0, 1) if kind == 1 else ():
            pairs = rows_of[date] // 2
            late = (HALO[date] + 1) // 2
            count = pairs - late if kind == 0 else late
            low_first = 0 if kind == 0 else pairs - late
            first = jnp.where(upper, pairs - count - low_first, low_first)

            def body(i, carry):
                lateral_pair(date, first + i)
                return carry

            lax.fori_loop(0, count, body, 0, unroll=True)
        if kind == 0:
            for copy in conv_copies[0]:
                copy.wait()
        for date in (0, 1):
            pairs = rows_of[date] // 2 - 1
            late = (HALO[date] + 1) // 2
            count = pairs - late if kind == 0 else late
            low_first = 0 if kind == 0 else pairs - late
            first = jnp.where(upper, pairs - count - low_first, low_first)

            def body(i, carry):
                pyramid_pairs(date, first + 2 * i, 2)
                return carry

            pyramid_pairs(date, first, count)

    for copy in lat_copies:
        copy.wait()
    lat_bias = vec_lat[...]
    for date in (0, 1):

        @pl.when(d == date)
        def _():
            own_copy(date).wait()
            lateral_core(date)

    for date in (0, 1):

        @pl.when(d != date)
        def _():
            await_kind(0, (0,), (date,))
            lateral_core(date)

    await_kind(0, (-1, 1))
    for date in (0, 1):
        lateral_sides(date)
    phase(0)

    tiles = []
    for kind in (0, 1):
        tile_row = r if kind == 0 else jnp.clip(other_row, 0, row_tiles - 1)
        for step in (0, -1, 1):
            tile_col = jnp.clip(c + step, 0, col_tiles - 1)
            ok = has_col[step]
            if kind == 1:
                ok = ok & has_other
            tiles.append((kind, step, ok, shift_ref[tile_col, 0, tile_row], shift_ref[tile_col, 1, tile_row]))
    reach = HALO[1] - 1
    x_left = x_mid[0 : 2 * SIDE]
    x_right = x_mid[mid - 2 * SIDE : mid]

    def regrid_row(p, slot):
        y = 2 * p + slot - 2
        sums = {0: 0.0, -1: 0.0, 1: 0.0}
        seen = {0: 0.0, -1: 0.0, 1: 0.0}
        for kind, step, ok, row_by, col_by in tiles:
            u = y + d * half - row_by
            within = (u >= 0) & (u < tile_rows)
            use = ok & (within if kind == 0 else jnp.logical_not(within))
            if step == 0:
                x, start, size = x_mid, 0, mid
                low, high = col_by, tile_cols + col_by
            elif step == -1:
                x, start, size = x_left, 0, 2 * SIDE
                low, high = -far, col_by
            else:
                x, start, size = x_right, mid - 2 * SIDE, 2 * SIDE
                low, high = tile_cols + col_by, far
            mask = (x >= low) & (x < jnp.where(use, high, -2 * far))
            piece = pyr_b[y - row_by + reach, pl.ds(start + edge - col_by, size), :]
            sums[step] = sums[step] + jnp.where(mask, piece, 0.0)
            seen[step] = seen[step] + jnp.where(mask, 1.0, 0.0)

        def whole(parts):
            full = parts[0]
            return jnp.concatenate(
                [
                    full[0 : 2 * SIDE] + parts[-1],
                    full[2 * SIDE : mid - 2 * SIDE],
                    full[mid - 2 * SIDE :] + parts[1],
                ],
                axis=0,
            )

        total, cover = whole(sums), whole(seen)
        placed = total / jnp.maximum(cover, 1.0)
        diff = jnp.abs(pyr_a[2 * p + slot] - placed) * jnp.minimum(cover, 1.0)
        diff = jnp.where(inside(x_mid, y), diff, 0.0)
        put_taps(dif6, p, slot, diff, 0, mid)

    def regrid_body(p, carry):
        regrid_row(p, 0)
        regrid_row(p, 1)
        return carry

    for copy in conv_copies[1]:
        copy.wait()
    bias_one = vec_one[...]

    def dec_one(i, count):
        value = conv_pairs(dif6, wd1, i, count)
        for pair in range(count):
            for slot in (0, 1):
                part = value[pair * mid : (pair + 1) * mid, slot * ch : (slot + 1) * ch]
                part = jnp.maximum(part + bias_one, 0.0)
                part = jnp.where(inside(x_mid, 2 * (i + pair) + slot - 1), part, 0.0)
                put_taps(hid6, i + pair, slot, part, edge, mid - edge)

    pairs = half // 2 + 2
    early = pairs - (HALO[1] + 1) // 2
    first = jnp.where(upper, pairs - early, 0)
    for i in range(early):
        regrid_body(first + i, 0)
    dec_one(jnp.where(upper, pairs - early, 0), early - 1)
    await_kind(1)
    phase(1)
    first = jnp.where(upper, 0, early)
    for i in range(pairs - early):
        regrid_body(first + i, 0)
    dec_one(jnp.where(upper, 0, early - 1), pairs - early)

    for copy in conv_copies[2]:
        copy.wait()
    bias_two = vec_two[...]
    out_w = jnp.broadcast_to(vec_out[...].astype(F32), (16, ch)).astype(BF16)
    out_b = b_out[0]
    for i in range(0, half // 2, half // 2):
        value = conv_pairs(hid6, wd2, i, half // 2)
        for pair in range(half // 2):
            for slot in (0, 1):
                part = value[pair * tile_cols : (pair + 1) * tile_cols, slot * ch : (slot + 1) * ch]
                part = jnp.maximum(part + bias_two, 0.0).astype(BF16)
                logit = lax.dot_general(
                    out_w, part, (((1,), (1,)), ((), ())), preferred_element_type=F32
                )
                y = 2 * (i + pair) + slot
                out_ref[y : y + 1, :] = logit[0:1] + out_b

    for date in (0, 1):

        @pl.when(d == date)
        def _():
            for go, copy in pieces(date):

                @pl.when(go)
                def _():
                    copy.wait_send()


def per_device(
    features, scene_shift, w_lat, b_lat, w_fpn, w_dec1, b_dec1, w_dec2, b_dec2, w_out, b_out
):
    tile_rows, tile_cols, ch = features.shape[1:]
    half = tile_rows // 2
    sizes = (lax.axis_size("rows"), lax.axis_size("cols"), tile_rows, tile_cols)
    rows_of = tuple(half + 2 * h for h in HALO)
    mid = tile_cols + 2 * SIDE
    hbm = pl.BlockSpec(memory_space=pltpu.HBM)
    vmem = pl.BlockSpec(memory_space=pltpu.VMEM)
    smem = pl.BlockSpec(memory_space=pltpu.SMEM)
    flops = 2 * ch * ch * tile_cols * 9 * 60
    return pl.pallas_call(
        functools.partial(kernel, sizes),
        out_shape=pltpu.VMEM((half, tile_cols), F32),
        in_specs=[
            hbm,
            smem,
            hbm,
            hbm,
            hbm,
            hbm,
            hbm,
            hbm,
            hbm,
            hbm,
            smem,
        ],
        out_specs=vmem,
        scratch_shapes=[
            pltpu.VMEM((sum(rows_of), mid // SIDE, SIDE, ch), BF16),
            pltpu.VMEM((sum(rows_of) // 2, mid, 6 * ch), BF16),
            pltpu.VMEM((half + 4, mid, ch), F32),
            pltpu.VMEM((half + 2 * HALO[1] - 2, mid + 2 * SIDE, ch), F32),
            pltpu.VMEM((half // 2 + 2, mid, 6 * ch), BF16),
            pltpu.VMEM((half // 2 + 1, tile_cols, 6 * ch), BF16),
            pltpu.VMEM((2 * ch, 2 * ch), BF16),
            pltpu.VMEM((12 * ch, 2 * ch), BF16),
            pltpu.VMEM((12 * ch, 2 * ch), BF16),
            pltpu.VMEM((12 * ch, 2 * ch), BF16),
            pltpu.VMEM((1, ch), F32),
            pltpu.VMEM((1, ch), F32),
            pltpu.VMEM((1, ch), F32),
            pltpu.VMEM((1, ch), BF16),
            pltpu.SemaphoreType.DMA((4, 3)),
            pltpu.SemaphoreType.DMA((2, 2, 3)),
            pltpu.SemaphoreType.DMA((12,)),
        ],
        compiler_params=pltpu.CompilerParams(
            collective_id=0, has_side_effects=True, vmem_limit_bytes=60 << 20
        ),
        cost_estimate=pl.CostEstimate(flops=flops, bytes_accessed=4 << 20, transcendentals=0),
    )(
        features.reshape(tile_rows, tile_cols // SIDE, SIDE, ch),
        scene_shift.transpose(1, 2, 0),
        w_lat,
        b_lat.reshape(1, ch),
        w_fpn.reshape(9 * ch, ch),
        w_dec1.reshape(9 * ch, ch),
        b_dec1.reshape(1, ch),
        w_dec2.reshape(9 * ch, ch),
        b_dec2.reshape(1, ch),
        w_out.reshape(1, ch),
        b_out,
    )


def solution(mesh):
    return jax.shard_map(
        per_device,
        mesh=mesh,
        in_specs=(
            P("date", ("groups", "rows"), "cols", None),
            P("groups", None, None),
            P(),
            P(),
            P(),
            P(),
            P(),
            P(),
            P(),
            P(),
            P(),
        ),
        out_specs=P(("groups", "rows", "date"), "cols"),
        check_vma=False,
    )
```
